512 devices in a mesh: section: 16 (over z), expert: 32 (over y, x, core).
Axes of the slice: x: 4, y: 4, z: 16, core: 2. Of those that a mesh axis runs over, the one named last changes fastest.
Arguments:
- tokens: bfloat16 [8, 256, 2048], P(None, 'expert', 'section'), may hold values from -6 to 6
- norm_gain: float32 [16, 2048], P('section'), may hold values from 0.1 to 1.9
- gate_weight: bfloat16 [16, 32, 2048, 384], P('section', 'expert'), may hold values from -0.125 to 0.125
- up_weight: bfloat16 [16, 32, 2048, 384], P('section', 'expert'), may hold values from -0.125 to 0.125
- down_weight: bfloat16 [16, 32, 384, 2048], P('section', 'expert'), may hold values from -0.3125 to 0.3125
- expert_ids: int32 [16, 8, 256, 8], P('section', None, 'expert'), may hold values from 0 to 31, all different within a row; in each aligned block of 8 rows (0 to 7, 8 to 15, ..., all dimensions but the last counted through in order) at most 2 rows name the same one
- gate_probs: float32 [16, 8, 256, 8], P('section', None, 'expert'), may hold values from 0.05 to 1
Outputs:
- hidden_states: bfloat16 [16, 8, 256, 2048], P('section', None, 'expert')
The draws below stay inside these ranges and needn't reach their ends.
Inputs may be any that keep to these rules, and one draw needn't show every extreme that they name: `expert_ids`: in the 8 rows of one index of expert for one layer and micro-batch (aligned blocks of 8 rows), no expert is named by more than 2 rows, a bound that some block reaches in every draw.
All inputs are finite; a program needn't handle non-finite values.
Results may differ from the reference program's by a relative error of at most 0.04.
Values may be sent and summed in bfloat16 or wider, within the bound.
No kernel may reach another device: no remote copies, remote signals or barrier semaphores. Data moves between devices by JAX's collectives and lax.ppermute only.
A program may use at most 64 MiB of HBM per device.

```python
import math
import jax
import jax.numpy as jnp
import numpy as np
from jax import lax

D = 2048
TOP = 8
FF = 384
EXPERTS = 32
MB = 8
ROWS_DEV = 8
CAP = 2
LAYERS = 16
TOKENS_MB = 256
N_EXPERT = 32


def levels(key, shape, split, low, high):
    loudness = 1.0
    for dim, parts in split:
        steps = jax.random.uniform(jax.random.fold_in(jax.random.fold_in(key, 6), dim), (parts,), jnp.float32, low / len(split), high / len(split))
        loudness = loudness * jnp.repeat(jnp.exp(steps), shape[dim] // parts).reshape((-1,) + (1,) * (len(shape) - 1 - dim))
    return loudness


def routed_block(rng, own, number, rows, count, top, bound, lean):
    ranking = jax.random.permutation(rng, count)
    crowded, ordinary = shares(count, rows * top, bound, lean, True), shares(count, rows * top, bound, lean, False)
    places = jnp.arange(count)

    def named(lengths, offset_by):
        used = int((lengths > 0).sum())
        fixed = max(1, used // 4)
        passed = fixed + (places - fixed + offset_by * (used - fixed)) % max(1, count - fixed)
        return jnp.zeros((count,), jnp.int32).at[ranking[jnp.where(places < fixed, places, passed)]].set(jnp.asarray(lengths, jnp.int32))

    lengths = jnp.where(number % 4 == 0, named(crowded, number // 4), named(ordinary, number - number // 4 - 1))
    mixed = jax.random.permutation(jax.random.fold_in(own, 3), count)
    giver, taker = mixed[0:count // 2 * 2:2], mixed[1:count // 2 * 2:2]
    margin = jnp.minimum(lengths[giver] - 1, bound - lengths[taker]) // 2
    margin = jnp.where((giver == ranking[0]) | (taker == ranking[0]) | (lengths[taker] == 0), 0, jnp.maximum(margin, 0))
    passed = jax.random.randint(jax.random.fold_in(own, 4), (count // 2,), 0, 1 << 20) % (margin + 1)
    lengths = lengths.at[giver].add(-passed).at[taker].add(passed)
    labels = jnp.searchsorted(jnp.cumsum(lengths), jnp.arange(rows * top), side="right").astype(jnp.int32)
    grid = labels.reshape(top, rows).T
    grid = grid[jax.random.permutation(jax.random.fold_in(own, 1), rows)]
    offset_by = jax.random.randint(jax.random.fold_in(own, 2), (rows, 1), 0, top)
    return jnp.take_along_axis(grid, (jnp.arange(top)[None, :] + offset_by) % top, axis=1)


def shares(amount, total, reach, slope, full):
    weights = [(1 << 20) // math.isqrt(standing ** slope) + 1 for standing in range(1, amount + 1)]
    largest = reach if full else min(reach, max(-(-total // amount), total * weights[0] // sum(weights)))
    least = 1 if total - largest >= amount - 1 else 0
    counts, spare = [largest] + [least] * (amount - 1), total - largest - least * (amount - 1)
    while spare > 0:
        movable = [i for i in range(1, amount) if counts[i] < largest] or [i for i in range(1, amount) if counts[i] < reach]
        mass, remaining = sum([weights[i] for i in movable]), spare
        for i in movable:
            addition = min(reach - counts[i], max(1, remaining * weights[i] // mass), spare)
            counts[i] = counts[i] + addition
            spare = spare - addition
    return np.array(counts)


def centred(rng, extent, spread, bound, shards=(), kind=jnp.bfloat16):
    result = spread * jax.random.normal(rng, extent, jnp.float32)
    if shards:
        result = result * levels(rng, extent, shards, -0.22, 0.18)
    return jnp.clip(result, -bound, bound).astype(kind)


def setup_inputs(seed: int = 0) -> dict:
    splits = jax.random.split(jax.random.key(seed), 8)
    tokens = centred(splits[0], (MB, TOKENS_MB, D), 1.0, 6.0, ((1, 32), (2, 16)))
    norm_gain = jnp.clip(1.0 + 0.18 * jax.random.normal(splits[1], (LAYERS, D), jnp.float32), 0.1, 1.9)
    gate_weight = centred(splits[2], (LAYERS, EXPERTS, D, FF), D ** -0.5, 0.125, ((0, 16), (1, 32)))
    up_weight = centred(splits[3], (LAYERS, EXPERTS, D, FF), D ** -0.5, 0.125, ((0, 16), (1, 32)))
    down_weight = centred(splits[4], (LAYERS, EXPERTS, FF, D), FF ** -0.5, 0.3125, ((0, 16), (1, 32)))
    expert_ids_keys = jax.random.split(jax.random.fold_in(splits[5], 1), LAYERS * MB * TOKENS_MB // ROWS_DEV)
    expert_ids_turns = jax.random.permutation(jax.random.fold_in(splits[5], 3), LAYERS * MB * TOKENS_MB // ROWS_DEV)
    expert_ids = jax.vmap(lambda own, number: routed_block(jax.random.fold_in(splits[5], 2), own, number, ROWS_DEV, EXPERTS, TOP, CAP, 2))(expert_ids_keys, expert_ids_turns).reshape((LAYERS, MB, TOKENS_MB, TOP))
    gate_probs = jnp.clip(jnp.exp(math.log(1.0) - 2.9957323 * jax.random.uniform(splits[6], (LAYERS, MB, TOKENS_MB, TOP), jnp.float32) ** levels(splits[6], (LAYERS, MB, TOKENS_MB, TOP), ((0, 16), (2, 32)), -0.2, 0.2)), 0.05, 1.0)
    return {"tokens": tokens, "norm_gain": norm_gain, "gate_weight": gate_weight, "up_weight": up_weight, "down_weight": down_weight, "expert_ids": expert_ids, "gate_probs": gate_probs}


EPS = 1e-06

def expert_rows(args):
    routed, w_gate, w_up, w_down = args
    gate_proj = jnp.dot(routed, w_gate, preferred_element_type=jnp.float32)
    up_proj = jnp.dot(routed, w_up, preferred_element_type=jnp.float32)
    active = (jax.nn.silu(gate_proj) * up_proj).astype(jnp.bfloat16)
    return jnp.dot(active, w_down, preferred_element_type=jnp.float32).astype(jnp.bfloat16)

def slot_numbers(flat_ids):
    onehot = (flat_ids[:, :, None] == jnp.arange(EXPERTS, dtype=jnp.int32)[None, None, :]).astype(jnp.int32)
    before = jnp.cumsum(onehot, axis=1) - onehot
    return flat_ids * CAP + lax.optimization_barrier(jnp.sum(onehot * before, axis=2))

def moe_layer(layer_input, norm_scale, expert_list, gate_share, w_gate, w_up, w_down):
    total_rows = layer_input.shape[0]
    blocks = N_EXPERT
    row_count = total_rows // blocks
    top_count = expert_list.shape[1]
    widened = layer_input.astype(jnp.float32)
    normed = (widened * lax.rsqrt(lax.optimization_barrier(jnp.mean(widened * widened, axis=-1, keepdims=True)) + EPS) * norm_scale).astype(jnp.bfloat16)
    weight = gate_share / lax.optimization_barrier(jnp.sum(gate_share, axis=-1, keepdims=True))
    slot_index = slot_numbers(expert_list.reshape(blocks, row_count * top_count)).reshape(blocks, row_count, top_count)
    target = jnp.arange(EXPERTS * CAP, dtype=jnp.int32)
    placement = lax.optimization_barrier(jnp.sum((slot_index[:, None, :, :] == target[None, :, None, None]).astype(jnp.float32), axis=3))
    normed_blocks = normed.astype(jnp.float32).reshape(blocks, row_count, D)
    buffer = jnp.einsum('bjr,brd->bjd', placement, normed_blocks, precision=lax.Precision.HIGHEST)
    buffer = buffer.reshape(blocks, EXPERTS, CAP, D).transpose(1, 0, 2, 3).reshape(EXPERTS, blocks * CAP, D).astype(jnp.bfloat16)
    outputs = lax.map(expert_rows, (buffer, w_gate, w_up, w_down))
    flat_out = outputs.reshape(EXPERTS * blocks * CAP, D)
    block_of = (jnp.arange(total_rows, dtype=jnp.int32) // row_count)[:, None]
    position = slot_index.reshape(total_rows, top_count) - expert_list * CAP
    index = (expert_list * (blocks * CAP) + block_of * CAP + position).astype(jnp.int32)
    picked = jnp.take(flat_out, index.reshape(-1), axis=0).astype(jnp.float32).reshape(total_rows, top_count, D)
    mixed = lax.optimization_barrier(jnp.sum(weight[:, :, None] * picked, axis=1))
    return (widened + mixed).astype(jnp.bfloat16)

def reference(tokens, norm_gain, gate_weight, up_weight, down_weight, expert_ids, gate_probs):
    current = tokens
    collected = []
    for layer_index in range(LAYERS):
        outputs = []
        for micro_index in range(MB):
            outputs.append(moe_layer(current[micro_index], norm_gain[layer_index], expert_ids[layer_index, micro_index], gate_probs[layer_index, micro_index], gate_weight[layer_index], up_weight[layer_index], down_weight[layer_index]))
        current = jnp.stack(outputs)
        collected.append(current)
    return jnp.stack(collected)
```

```python
import jax
import jax.numpy as jnp
from jax import lax
from jax.sharding import PartitionSpec as P

CAP = 2


EPS = 1e-06


def passed_along(value, axis, by):
    length = lax.axis_size(axis)
    pairs = [(i, i + by) for i in range(length) if 0 <= i + by < length]
    return lax.ppermute(value, axis, pairs)


def expert_block(routed, w_gate, w_up, w_down):
    gate_proj = jnp.einsum("escd,edf->escf", routed, w_gate, preferred_element_type=jnp.float32)
    up_proj = jnp.einsum("escd,edf->escf", routed, w_up, preferred_element_type=jnp.float32)
    active = (jax.nn.silu(gate_proj) * up_proj).astype(jnp.bfloat16)
    return jnp.einsum("escf,efd->escd", active, w_down, preferred_element_type=jnp.float32).astype(
        jnp.bfloat16
    )


def slot_numbers(expert_list, capacity):
    same = (expert_list[:, None, :, None] == expert_list[None, :, None, :]).any(axis=3)
    rows = jnp.arange(expert_list.shape[0])
    earlier = same & (rows[None, :] < rows[:, None])[:, :, None]
    return expert_list * capacity + jnp.sum(earlier.astype(jnp.int32), axis=1)


def moe_layer(layer_input, norm_scale, expert_list, gate_share, w_gate, w_up, w_down):
    row_count, columns = layer_input.shape
    experts_local = w_gate.shape[0]
    groups = lax.axis_size("expert")
    experts = experts_local * groups
    capacity = CAP
    widened = layer_input.astype(jnp.float32)
    normed = (
        widened * lax.rsqrt(jnp.mean(widened * widened, axis=-1, keepdims=True) + EPS) * norm_scale
    ).astype(jnp.bfloat16)
    weight = gate_share / jnp.sum(gate_share, axis=-1, keepdims=True)
    slot_index = slot_numbers(expert_list, capacity)
    target = jnp.arange(experts * capacity, dtype=jnp.int32)
    placement = jnp.sum(
        (slot_index[None, :, :] == target[:, None, None]).astype(jnp.bfloat16), axis=2
    )
    sending = jnp.dot(placement, normed, preferred_element_type=jnp.float32).astype(jnp.bfloat16)
    sending = sending.reshape(experts, 1, capacity, columns)
    results = expert_block(
        lax.all_to_all(sending, "expert", split_axis=0, concat_axis=1, tiled=True),
        w_gate,
        w_up,
        w_down,
    )
    returned = lax.all_to_all(results, "expert", split_axis=1, concat_axis=0, tiled=True)
    returns_wide = returned.reshape(experts * capacity, columns).astype(jnp.float32)
    mixing = jnp.sum(
        (slot_index[:, :, None] == target[None, None, :]).astype(jnp.float32) * weight[:, :, None],
        axis=1,
    )
    mixed = jnp.dot(mixing, returns_wide, precision=lax.Precision.HIGHEST)
    return (widened + mixed).astype(jnp.bfloat16)


def local(tokens, norm_gain, gate_weight, up_weight, down_weight, expert_ids, gate_probs):
    section_index = lax.axis_index("section")
    section_count = lax.axis_size("section")
    full_tokens = lax.all_gather(tokens, "section", axis=2, tiled=True)
    micro_count, row_count, columns = full_tokens.shape
    turn_count = section_count + micro_count - 1
    norm_scale = norm_gain[0]
    w_gate = gate_weight[0]
    w_up = up_weight[0]
    w_down = down_weight[0]
    layer_ids = expert_ids[0]
    layer_probs = gate_probs[0]

    def advance(turn_index, state_pair):
        incoming, hidden_out = state_pair
        micro_index = turn_index - section_index
        is_valid = (micro_index >= 0) & (micro_index < micro_count)
        micro_pick = jnp.clip(micro_index, 0, micro_count - 1)
        fresh_rows = lax.dynamic_index_in_dim(full_tokens, micro_pick, 0, keepdims=False)
        layer_input = jnp.where(section_index == 0, fresh_rows, incoming)
        expert_list = lax.dynamic_index_in_dim(layer_ids, micro_pick, 0, keepdims=False)
        gate_share = lax.dynamic_index_in_dim(layer_probs, micro_pick, 0, keepdims=False)
        layer_output = moe_layer(
            layer_input, norm_scale, expert_list, gate_share, w_gate, w_up, w_down
        )
        updated = lax.dynamic_update_index_in_dim(hidden_out, layer_output, micro_pick, 0)
        hidden_out = jnp.where(is_valid, updated, hidden_out)
        passed = passed_along(layer_output, "section", 1)
        return (passed, hidden_out)

    initial = (
        jnp.zeros((row_count, columns), jnp.bfloat16),
        jnp.zeros((micro_count, row_count, columns), jnp.bfloat16),
    )
    final_pair = lax.fori_loop(0, turn_count, advance, initial)
    return final_pair[1][None]


def solution(mesh):
    in_specs = (
        P(None, "expert", "section"),
        P("section", None),
        P("section", "expert", None, None),
        P("section", "expert", None, None),
        P("section", "expert", None, None),
        P("section", None, "expert", None),
        P("section", None, "expert", None),
    )
    out_specs = P("section", None, "expert", None)
    return jax.shard_map(local, mesh=mesh, in_specs=in_specs, out_specs=out_specs, check_vma=False)
```

```python
import jax
import jax.numpy as jnp
from jax import lax
from jax.experimental import pallas as pl
from jax.experimental.pallas import tpu as pltpu
from jax.sharding import PartitionSpec as P

CAP = 2
EPS = 1e-06
LANES = 128
GROUP = 2

VMEM = pl.BlockSpec(memory_space=pltpu.VMEM)
SMEM = pl.BlockSpec(memory_space=pltpu.SMEM)


def place_kernel(turn_ref, row_ref, x_ref, gain_ref, send_ref, normed_ref):
    experts, slots, parts, lanes = send_ref.shape
    wide = x_ref[...].astype(jnp.float32)
    mean = jnp.sum(wide * wide, axis=(1, 2), keepdims=True) * (1.0 / (parts * lanes))
    normed = wide * lax.rsqrt(mean + EPS) * gain_ref[...][None]
    normed_ref[...] = normed.astype(jnp.bfloat16)
    pick = turn_ref[0]
    for e in range(experts):
        for q in range(slots):
            send_ref[e, q] = normed_ref[row_ref[pick, e * slots + q]]


def expert_kernel(recv_ref, gate_ref, up_ref, down_ref, out_ref, wide_ref):
    rows, parts, lanes = recv_ref.shape
    wide_ref[...] = recv_ref[...].astype(jnp.float32).reshape(rows * parts, lanes)
    routed = jnp.concatenate(
        [wide_ref[pl.ds(c, rows, stride=parts), :].astype(jnp.bfloat16) for c in range(parts)],
        axis=1,
    )
    gate = jnp.dot(routed, gate_ref[...], preferred_element_type=jnp.float32)
    up = jnp.dot(routed, up_ref[...], preferred_element_type=jnp.float32)
    active = (gate / (1.0 + jnp.exp(-gate)) * up).astype(jnp.bfloat16)
    result = jnp.dot(active, down_ref[...], preferred_element_type=jnp.float32)
    for c in range(parts):
        wide_ref[pl.ds(c, rows, stride=parts), :] = result[:, c * lanes : (c + 1) * lanes]
    out_ref[...] = wide_ref[...].reshape(rows, parts, lanes).astype(jnp.bfloat16)


def mix_kernel(turn_ref, slot_ref, share_ref, ret_ref, x_ref, out_ref):
    rows = x_ref.shape[0]
    top = slot_ref.shape[1] // rows
    pick = turn_ref[0]
    for r in range(rows):
        total = x_ref[r].astype(jnp.float32)
        for k in range(top):
            part = ret_ref[slot_ref[pick, r * top + k]].astype(jnp.float32)
            total = total + share_ref[pick, r * top + k] * part
        out_ref[r] = total.astype(jnp.bfloat16)


def tables(expert_list, gate_probs, experts):
    micro, rows, _ = expert_list.shape
    groups = micro // GROUP
    number = jnp.arange(rows)
    member = (jnp.arange(micro) % GROUP)[:, None, None]
    chosen = expert_list[..., None] == jnp.arange(experts)
    named = chosen.any(axis=2)
    first = jnp.min(jnp.where(named, number[None, :, None], rows - 1), axis=1)
    last = jnp.max(jnp.where(named, number[None, :, None], 0), axis=1)
    later = chosen & (first[:, None, None, :] < number[None, :, None, None])
    rank = jnp.sum(later.astype(jnp.int32), axis=3)
    slot = expert_list * (CAP * GROUP) + member * CAP + rank
    source = jnp.stack([first, last], axis=2) + member * rows
    source = source.reshape(groups, GROUP, experts, CAP).transpose(0, 2, 1, 3)
    share = gate_probs / jnp.sum(gate_probs, axis=-1, keepdims=True)
    spare = lambda a: jnp.pad(a.reshape(groups, -1), ((0, 1), (0, 0)))
    return spare(source), spare(slot), spare(share)


def local(tokens, norm_gain, gate_weight, up_weight, down_weight, expert_ids, gate_probs):
    section = lax.axis_index("section")
    sections = lax.axis_size("section")
    experts = lax.axis_size("expert")
    micro, rows_one, lanes = tokens.shape
    groups = micro // GROUP
    rows = rows_one * GROUP
    parts = sections
    slots = CAP * GROUP
    turns = sections + groups - 1
    source, slot, share = tables(expert_ids[0], gate_probs[0], experts)
    gain = norm_gain.reshape(parts, lanes)
    w_gate, w_up, w_down = gate_weight[0, 0], up_weight[0, 0], down_weight[0, 0]

    grouped = tokens.reshape(groups, rows, lanes)
    held = jnp.concatenate([grouped[:1], grouped[:0:-1]])
    held = jnp.tile(held, (sections // groups, 1, 1))
    held = lax.all_to_all(held, "section", split_axis=0, concat_axis=0, tiled=True)
    held = held.transpose(1, 0, 2)

    params = pltpu.CompilerParams(vmem_limit_bytes=24 * 1024 * 1024)
    bf = lambda *shape: jax.ShapeDtypeStruct(shape, jnp.bfloat16)
    place = pl.pallas_call(
        place_kernel,
        out_shape=bf(experts, slots, parts, lanes),
        in_specs=[SMEM, SMEM, VMEM, VMEM],
        out_specs=VMEM,
        scratch_shapes=[pltpu.VMEM((rows, parts, lanes), jnp.bfloat16)],
        compiler_params=params,
        name="place",
    )
    expert = pl.pallas_call(
        expert_kernel,
        out_shape=bf(experts * slots, parts, lanes),
        in_specs=[VMEM] * 4,
        out_specs=VMEM,
        scratch_shapes=[pltpu.VMEM((experts * slots * parts, lanes), jnp.float32)],
        compiler_params=params,
        name="expert",
    )
    mix = pl.pallas_call(
        mix_kernel,
        out_shape=bf(rows, parts, lanes),
        in_specs=[SMEM, SMEM, SMEM, VMEM, VMEM],
        out_specs=VMEM,
        compiler_params=params,
        name="mix",
    )
    exchange = lambda a: lax.all_to_all(a, "expert", split_axis=0, concat_axis=0, tiled=True)
    ring = [(i, (i + 1) % sections) for i in range(sections)]

    def layer(turn, held, hidden):
        index = turn - section
        pick = jnp.where((index >= 0) & (index < groups), index, groups).astype(jnp.int32)
        at = pick.reshape(1)
        sent = place(at, source, held, gain)
        arrived = exchange(sent.reshape(experts, slots * parts, lanes))
        results = expert(arrived.reshape(experts * slots, parts, lanes), w_gate, w_up, w_down)
        returned = exchange(results.reshape(experts, slots * parts, lanes))
        output = mix(at, slot, share, returned.reshape(experts * slots, parts, lanes), held)
        return output, lax.dynamic_update_index_in_dim(hidden, output, pick, 0)

    def advance(turn, state):
        output, hidden = layer(turn, *state)
        return lax.ppermute(output, "section", ring), hidden

    hidden = jnp.zeros((groups + 1, rows, parts, lanes), jnp.bfloat16)
    state = lax.fori_loop(0, turns - 1, advance, (held, hidden))
    _, hidden = layer(turns - 1, *state)
    return hidden[:groups].reshape(1, micro, rows_one, parts * lanes)


def solution(mesh):
    in_specs = (
        P(None, "expert", "section"),
        P("section", None),
        P("section", "expert", None, None),
        P("section", "expert", None, None),
        P("section", "expert", None, None),
        P("section", None, "expert", None),
        P("section", None, "expert", None),
    )
    out_specs = P("section", None, "expert", None)
    return jax.shard_map(local, mesh=mesh, in_specs=in_specs, out_specs=out_specs, check_vma=False)
```

```python
import functools

import jax
import jax.numpy as jnp
from jax import lax
from jax.experimental import pallas as pl
from jax.experimental.pallas import tpu as pltpu
from jax.sharding import PartitionSpec as P

CAP = 2
EPS = 1e-06
LANES = 128
GROUP = 2

VMEM = pl.BlockSpec(memory_space=pltpu.VMEM)
SMEM = pl.BlockSpec(memory_space=pltpu.SMEM)
ANY = pl.BlockSpec(memory_space=pl.ANY)


def place_kernel(turn_ref, row_ref, x_ref, gain_ref, send_ref, normed_ref):
    experts, slots, parts, lanes = send_ref.shape
    wide = x_ref[...].astype(jnp.float32)
    mean = jnp.sum(wide * wide, axis=(1, 2), keepdims=True) * (1.0 / (parts * lanes))
    normed = wide * lax.rsqrt(mean + EPS) * gain_ref[...][None]
    normed_ref[...] = normed.astype(jnp.bfloat16)
    pick = turn_ref[0]
    for e in range(experts):
        for q in range(slots):
            send_ref[e, q] = normed_ref[row_ref[pick, e * slots + q]]


def expert_kernel(own_ref, recv_ref, *refs):
    out_ref, gate_ref, up_ref, down_ref, wide_ref, sems = refs[-6:]
    weights, held = refs[:-6], (gate_ref, up_ref, down_ref)
    rows, parts, lanes = recv_ref.shape
    copies = [pltpu.make_async_copy(weights[i], held[i], sems.at[i]) for i in range(3)]
    if len(weights) == 3:
        for copy in copies:
            copy.start()
    else:

        @pl.when(own_ref[0] == 1)
        def _():
            for copy in copies:
                copy.start()

        @pl.when(own_ref[0] != 1)
        def _():
            for i in range(3):
                pltpu.make_async_copy(weights[3 + i], held[i], sems.at[i]).start()

    wide_ref[...] = recv_ref[...].astype(jnp.float32).reshape(rows * parts, lanes)
    routed = jnp.concatenate(
        [wide_ref[pl.ds(c, rows, stride=parts), :].astype(jnp.bfloat16) for c in range(parts)],
        axis=1,
    )
    copies[0].wait()
    gate = jnp.dot(routed, gate_ref[...], preferred_element_type=jnp.float32)
    copies[1].wait()
    up = jnp.dot(routed, up_ref[...], preferred_element_type=jnp.float32)
    active = (gate / (1.0 + jnp.exp(-gate)) * up).astype(jnp.bfloat16)
    copies[2].wait()
    result = jnp.dot(active, down_ref[...], preferred_element_type=jnp.float32)
    for c in range(parts):
        wide_ref[pl.ds(c, rows, stride=parts), :] = result[:, c * lanes : (c + 1) * lanes]
    out_ref[...] = wide_ref[...].reshape(rows, parts, lanes).astype(jnp.bfloat16)


def mix_kernel(turn_ref, slot_ref, share_ref, ret_ref, x_ref, out_ref):
    rows = x_ref.shape[0]
    top = slot_ref.shape[1] // rows
    pick = turn_ref[0]
    for r in range(rows):
        total = x_ref[r].astype(jnp.float32)
        for k in range(top):
            part = ret_ref[slot_ref[pick, r * top + k]].astype(jnp.float32)
            total = total + share_ref[pick, r * top + k] * part
        out_ref[r] = total.astype(jnp.bfloat16)


def tables(expert_list, gate_probs, experts):
    micro, rows, _ = expert_list.shape
    groups = micro // GROUP
    number = jnp.arange(rows)
    member = (jnp.arange(micro) % GROUP)[:, None, None]
    chosen = expert_list[..., None] == jnp.arange(experts)
    named = chosen.any(axis=2)
    first = jnp.min(jnp.where(named, number[None, :, None], rows - 1), axis=1)
    last = jnp.max(jnp.where(named, number[None, :, None], 0), axis=1)
    later = chosen & (first[:, None, None, :] < number[None, :, None, None])
    rank = jnp.sum(later.astype(jnp.int32), axis=3)
    slot = expert_list * (CAP * GROUP) + member * CAP + rank
    source = jnp.stack([first, last], axis=2) + member * rows
    source = source.reshape(groups, GROUP, experts, CAP).transpose(0, 2, 1, 3)
    share = gate_probs / jnp.sum(gate_probs, axis=-1, keepdims=True)
    spare = lambda a: jnp.pad(a.reshape(groups, -1), ((0, 1), (0, 0)))
    return spare(source), spare(slot), spare(share)


def local(tokens, norm_gain, gate_weight, up_weight, down_weight, expert_ids, gate_probs):
    section = lax.axis_index("section")
    sections = lax.axis_size("section")
    experts = lax.axis_size("expert")
    column, stage = section % 2, section // 2
    micro, rows_one, lanes = tokens.shape
    groups = micro // GROUP
    rows = rows_one * GROUP
    parts = sections
    slots = CAP * GROUP
    last = sections + groups - 2
    swap = [(i, i ^ 1) for i in range(sections)]

    fresh = jnp.broadcast_to(tokens.reshape(1, -1, lanes), (sections, micro * rows_one, lanes))
    fresh = lax.all_to_all(fresh, "section", split_axis=0, concat_axis=0, tiled=True)
    fresh = fresh.transpose(1, 0, 2).reshape(groups, rows, parts, lanes)

    source, slot, share = tables(expert_ids[0], gate_probs[0], experts)
    gain = norm_gain.reshape(parts, lanes)
    flat = lambda a: a.reshape(-1, lanes).astype(jnp.float32)
    packed = jnp.concatenate([flat(source), flat(slot), flat(share), gain])
    moved = lax.ppermute(packed, "section", swap)
    both = jnp.where(column == 0, jnp.stack([packed, moved]), jnp.stack([moved, packed]))
    size = source.size // lanes
    as_table = lambda a: a.reshape(2 * (groups + 1), -1)
    source = as_table(both[:, :size]).astype(jnp.int32)
    slot = as_table(both[:, size : 2 * size]).astype(jnp.int32)
    share = as_table(both[:, 2 * size : 3 * size])
    gains = both[:, 3 * size :].reshape(2 * parts, lanes)

    own_weights = (gate_weight[0, 0], up_weight[0, 0], down_weight[0, 0])
    ready, fresh, gains = lax.optimization_barrier((own_weights, fresh, gains))
    other_weights = tuple(lax.ppermute(w, "section", swap[2:]) for w in ready)

    params = pltpu.CompilerParams(vmem_limit_bytes=24 * 1024 * 1024)
    bf = lambda *shape: jax.ShapeDtypeStruct(shape, jnp.bfloat16)
    place = pl.pallas_call(
        place_kernel,
        out_shape=bf(experts, slots, parts, lanes),
        in_specs=[SMEM, SMEM, VMEM, VMEM],
        out_specs=VMEM,
        scratch_shapes=[pltpu.VMEM((rows, parts, lanes), jnp.bfloat16)],
        compiler_params=params,
        name="place",
    )
    def expert(own, arrived, *weights):
        return pl.pallas_call(
            expert_kernel,
            out_shape=bf(experts * slots, parts, lanes),
            in_specs=[SMEM, VMEM] + [ANY] * len(weights),
            out_specs=VMEM,
            scratch_shapes=[pltpu.VMEM(w.shape, jnp.bfloat16) for w in own_weights]
            + [
                pltpu.VMEM((experts * slots * parts, lanes), jnp.float32),
                pltpu.SemaphoreType.DMA((3,)),
            ],
            compiler_params=params,
            name="expert",
        )(own, arrived, *weights)

    mix = pl.pallas_call(
        mix_kernel,
        out_shape=bf(rows, parts, lanes),
        in_specs=[SMEM, SMEM, SMEM, VMEM, VMEM],
        out_specs=VMEM,
        compiler_params=params,
        name="mix",
    )
    exchange = lambda a: lax.all_to_all(a, "expert", split_axis=0, concat_axis=0, tiled=True)

    def layer(turn, held, hidden, weights):
        second = jnp.where(stage == 0, column, (turn - column) % 2)
        group = turn - 2 * stage - second
        active = (group >= 0) & (group < groups)
        pick = (jnp.where(active, group, groups) + second * (groups + 1)).astype(jnp.int32)
        own = ((stage == 0) | (second == column)).astype(jnp.int32).reshape(1)
        at = pick.reshape(1)
        gain_now = lax.dynamic_slice_in_dim(gains, second * parts, parts, 0)
        sent = place(at, source, held, gain_now)
        arrived = exchange(sent.reshape(experts, slots * parts, lanes))
        results = expert(own, arrived.reshape(experts * slots, parts, lanes), *weights)
        returned = exchange(results.reshape(experts, slots * parts, lanes))
        output = mix(at, slot, share, returned.reshape(experts * slots, parts, lanes), held)
        return output, lax.dynamic_update_index_in_dim(hidden, output, pick, 0)

    def move(value, pairs):
        here = functools.reduce(jnp.logical_or, [section == b for _, b in pairs])
        return jnp.where(here, lax.ppermute(value, "section", pairs), value)

    def opening_pairs(turn):
        pairs = [(0, 1)] if turn < groups else []
        pairs += [(1, 2 + (turn - 1) % 2)] if 1 <= turn <= groups else []
        for a in range(2, sections - 2):
            group = turn - (a // 2 * 2 + 1)
            if 0 <= group < groups and group % 2 == a % 2:
                pairs.append((a, a + 2))
        return pairs

    def steady_pairs(parity):
        return [(a, a + 2) for a in range(2 + parity, sections - 2, 2)]

    hidden = jnp.zeros((2 * (groups + 1), rows, parts, lanes), jnp.bfloat16)
    held = jnp.zeros((rows, parts, lanes), jnp.bfloat16)

    def entering(turn, held):
        group = lax.dynamic_index_in_dim(fresh, turn, 0, keepdims=False)
        return jnp.where(section == 0, group, held)

    def begin(turn, state):
        held, hidden = state
        held, hidden = layer(turn, entering(turn, held), hidden, own_weights)
        return move(held, opening_pairs(0) + opening_pairs(1)[1:]), hidden

    held, hidden = lax.fori_loop(0, 2, begin, (held, hidden))
    held, other_weights = lax.optimization_barrier((held, other_weights))
    all_weights = own_weights + other_weights
    for turn in range(2, groups + 1):
        if turn < groups:
            held = entering(turn, held)
        held, hidden = layer(turn, held, hidden, own_weights if turn < 3 else all_weights)
        held = move(held, opening_pairs(turn))

    def advance(i, state):
        held, hidden = state
        for step in range(2):
            turn = groups + 1 + 2 * i + step
            held, hidden = layer(turn, held, hidden, all_weights)
            held = move(held, steady_pairs((groups + 2 + step) % 2))
        return held, hidden

    held, hidden = lax.fori_loop(0, (last - 2 - groups) // 2, advance, (held, hidden))
    for turn in (last - 1, last):
        held, hidden = layer(turn, held, hidden, all_weights)

    low, high = hidden[:groups], hidden[groups + 1 : 2 * groups + 1]
    theirs = jnp.where(column == 0, high[0::2], low[1::2])
    theirs = lax.ppermute(theirs, "section", swap)
    mine = jnp.where(column == 0, low, high)
    result = [
        jnp.where((stage == 0) | (column == j % 2), mine[j], theirs[j // 2]) for j in range(groups)
    ]
    return jnp.stack(result).reshape(1, micro, rows_one, parts * lanes)


def solution(mesh):
    in_specs = (
        P(None, "expert", "section"),
        P("section", None),
        P("section", "expert", None, None),
        P("section", "expert", None, None),
        P("section", "expert", None, None),
        P("section", None, "expert", None),
        P("section", None, "expert", None),
    )
    out_specs = P("section", None, "expert", None)
    return jax.shard_map(local, mesh=mesh, in_specs=in_specs, out_specs=out_specs, check_vma=False)
```

```python
import functools

import jax
import jax.numpy as jnp
from jax import lax
from jax.experimental import pallas as pl
from jax.experimental.pallas import tpu as pltpu
from jax.sharding import PartitionSpec as P

CAP = 2
EPS = 1e-06
LANES = 128
GROUP = 2

VMEM = pl.BlockSpec(memory_space=pltpu.VMEM)
SMEM = pl.BlockSpec(memory_space=pltpu.SMEM)
ANY = pl.BlockSpec(memory_space=pl.ANY)


def place_kernel(turn_ref, row_ref, x_ref, gain_ref, send_ref, normed_ref):
    experts, slots, parts, lanes = send_ref.shape
    wide = x_ref[...].astype(jnp.float32)
    mean = jnp.sum(wide * wide, axis=(1, 2), keepdims=True) * (1.0 / (parts * lanes))
    normed = wide * lax.rsqrt(mean + EPS) * gain_ref[...][None]
    normed_ref[...] = normed.astype(jnp.bfloat16)
    pick = turn_ref[0]
    for e in range(experts):
        for q in range(slots):
            send_ref[e, q] = normed_ref[row_ref[pick, e * slots + q]]


def expert_kernel(own_ref, recv_ref, *refs):
    out_ref, gate_ref, up_ref, down_ref, wide_ref, sems = refs[-6:]
    weights, held = refs[:-6], (gate_ref, up_ref, down_ref)
    rows, parts, lanes = recv_ref.shape
    copies = [pltpu.make_async_copy(weights[i], held[i], sems.at[i]) for i in range(3)]
    if len(weights) == 3:
        for copy in copies:
            copy.start()
    else:

        @pl.when(own_ref[0] == 1)
        def _():
            for copy in copies:
                copy.start()

        @pl.when(own_ref[0] != 1)
        def _():
            for i in range(3):
                pltpu.make_async_copy(weights[3 + i], held[i], sems.at[i]).start()

    wide_ref[...] = recv_ref[...].astype(jnp.float32).reshape(rows * parts, lanes)
    routed = jnp.concatenate(
        [wide_ref[pl.ds(c, rows, stride=parts), :].astype(jnp.bfloat16) for c in range(parts)],
        axis=1,
    )
    copies[0].wait()
    gate = jnp.dot(routed, gate_ref[...], preferred_element_type=jnp.float32)
    copies[1].wait()
    up = jnp.dot(routed, up_ref[...], preferred_element_type=jnp.float32)
    active = (gate / (1.0 + jnp.exp(-gate)) * up).astype(jnp.bfloat16)
    copies[2].wait()
    result = jnp.dot(active, down_ref[...], preferred_element_type=jnp.float32)
    for c in range(parts):
        wide_ref[pl.ds(c, rows, stride=parts), :] = result[:, c * lanes : (c + 1) * lanes]
    out_ref[...] = wide_ref[...].reshape(rows, parts, lanes).astype(jnp.bfloat16)


def mix_kernel(turn_ref, slot_ref, share_ref, ret_ref, x_ref, out_ref):
    rows = x_ref.shape[0]
    top = slot_ref.shape[1] // rows
    pick = turn_ref[0]
    for r in range(rows):
        total = x_ref[r].astype(jnp.float32)
        for k in range(top):
            part = ret_ref[slot_ref[pick, r * top + k]].astype(jnp.float32)
            total = total + share_ref[pick, r * top + k] * part
        out_ref[r] = total.astype(jnp.bfloat16)


def tables(expert_list, gate_probs, experts):
    micro, rows, _ = expert_list.shape
    groups = micro // GROUP
    number = jnp.arange(rows)
    member = (jnp.arange(micro) % GROUP)[:, None, None]
    chosen = expert_list[..., None] == jnp.arange(experts)
    named = chosen.any(axis=2)
    first = jnp.min(jnp.where(named, number[None, :, None], rows - 1), axis=1)
    last = jnp.max(jnp.where(named, number[None, :, None], 0), axis=1)
    later = chosen & (first[:, None, None, :] < number[None, :, None, None])
    rank = jnp.sum(later.astype(jnp.int32), axis=3)
    slot = expert_list * (CAP * GROUP) + member * CAP + rank
    source = jnp.stack([first, last], axis=2) + member * rows
    source = source.reshape(groups, GROUP, experts, CAP).transpose(0, 2, 1, 3)
    share = gate_probs / jnp.sum(gate_probs, axis=-1, keepdims=True)
    spare = lambda a: jnp.pad(a.reshape(groups, -1), ((0, 1), (0, 0)))
    return spare(source), spare(slot), spare(share)


def local(tokens, norm_gain, gate_weight, up_weight, down_weight, expert_ids, gate_probs):
    section = lax.axis_index("section")
    sections = lax.axis_size("section")
    experts = lax.axis_size("expert")
    column, stage = section % 2, section // 2
    micro, rows_one, lanes = tokens.shape
    groups = micro // GROUP
    rows = rows_one * GROUP
    parts = sections
    slots = CAP * GROUP
    last = sections + groups - 2
    swap = [(i, i ^ 1) for i in range(sections)]

    fresh = jnp.broadcast_to(tokens.reshape(1, -1, lanes), (sections, micro * rows_one, lanes))
    fresh = lax.all_to_all(fresh, "section", split_axis=0, concat_axis=0, tiled=True)
    fresh = fresh.transpose(1, 0, 2).reshape(groups, rows, parts, lanes)

    source, slot, share = tables(expert_ids[0], gate_probs[0], experts)
    gain = norm_gain.reshape(parts, lanes)
    flat = lambda a: a.reshape(-1, lanes).astype(jnp.float32)
    packed = jnp.concatenate([flat(source), flat(slot), flat(share), gain])
    moved = lax.ppermute(packed, "section", swap)
    both = jnp.where(column == 0, jnp.stack([packed, moved]), jnp.stack([moved, packed]))
    size = source.size // lanes
    as_table = lambda a: a.reshape(2 * (groups + 1), -1)
    source = as_table(both[:, :size]).astype(jnp.int32)
    slot = as_table(both[:, size : 2 * size]).astype(jnp.int32)
    share = as_table(both[:, 2 * size : 3 * size])
    gains = both[:, 3 * size :].reshape(2 * parts, lanes)

    own_weights = (gate_weight[0, 0], up_weight[0, 0], down_weight[0, 0])
    ready, fresh, gains = lax.optimization_barrier((own_weights, fresh, gains))
    other_weights = tuple(lax.ppermute(w, "section", swap[2:]) for w in ready)

    params = pltpu.CompilerParams(vmem_limit_bytes=24 * 1024 * 1024)
    bf = lambda *shape: jax.ShapeDtypeStruct(shape, jnp.bfloat16)
    place = pl.pallas_call(
        place_kernel,
        out_shape=bf(experts, slots, parts, lanes),
        in_specs=[SMEM, SMEM, VMEM, VMEM],
        out_specs=VMEM,
        scratch_shapes=[pltpu.VMEM((rows, parts, lanes), jnp.bfloat16)],
        compiler_params=params,
        name="place",
    )
    def expert(own, arrived, *weights):
        return pl.pallas_call(
            expert_kernel,
            out_shape=bf(experts * slots, parts, lanes),
            in_specs=[SMEM, VMEM] + [ANY] * len(weights),
            out_specs=VMEM,
            scratch_shapes=[pltpu.VMEM(w.shape, jnp.bfloat16) for w in own_weights]
            + [
                pltpu.VMEM((experts * slots * parts, lanes), jnp.float32),
                pltpu.SemaphoreType.DMA((3,)),
            ],
            compiler_params=params,
            name="expert",
        )(own, arrived, *weights)

    mix = pl.pallas_call(
        mix_kernel,
        out_shape=bf(rows, parts, lanes),
        in_specs=[SMEM, SMEM, SMEM, VMEM, VMEM],
        out_specs=VMEM,
        compiler_params=params,
        name="mix",
    )
    exchange = lambda a: lax.all_to_all(a, "expert", split_axis=0, concat_axis=0, tiled=True)

    def layer(turn, held, hidden, weights):
        turn, held, hidden = lax.optimization_barrier((jnp.int32(turn), held, hidden))
        second = jnp.where(stage == 0, column, (turn - column) % 2)
        group = turn - 2 * stage - second
        active = (group >= 0) & (group < groups)
        pick = (jnp.where(active, group, groups) + second * (groups + 1)).astype(jnp.int32)
        own = ((stage == 0) | (second == column)).astype(jnp.int32).reshape(1)
        at = pick.reshape(1)
        gain_now = lax.dynamic_slice_in_dim(gains, second * parts, parts, 0)
        at, pick, own, gain_now, held, hidden = lax.optimization_barrier(
            (at, pick, own, gain_now, held, hidden)
        )
        sent = place(at, source, held, gain_now)
        arrived = exchange(sent.reshape(experts, slots * parts, lanes))
        results = expert(own, arrived.reshape(experts * slots, parts, lanes), *weights)
        returned = exchange(results.reshape(experts, slots * parts, lanes))
        returned, pick = lax.optimization_barrier((returned, pick))
        output = mix(at, slot, share, returned.reshape(experts * slots, parts, lanes), held)
        return output, lax.dynamic_update_index_in_dim(hidden, output, pick, 0)

    def move(value, pairs):
        here = functools.reduce(jnp.logical_or, [section == b for _, b in pairs])
        return jnp.where(here, lax.ppermute(value, "section", pairs), value)

    def opening_pairs(turn):
        pairs = [(0, 1)] if turn < groups else []
        pairs += [(1, 2 + (turn - 1) % 2)] if 1 <= turn <= groups else []
        for a in range(2, sections - 2):
            group = turn - (a // 2 * 2 + 1)
            if 0 <= group < groups and group % 2 == a % 2:
                pairs.append((a, a + 2))
        return pairs

    def steady_pairs(parity):
        return [(a, a + 2) for a in range(2 + parity, sections - 2, 2)]

    hidden = jnp.zeros((2 * (groups + 1), rows, parts, lanes), jnp.bfloat16)
    held = jnp.zeros((rows, parts, lanes), jnp.bfloat16)

    def entering(turn, held):
        group = lax.dynamic_index_in_dim(fresh, turn, 0, keepdims=False)
        return jnp.where(section == 0, group, held)

    def begin(turn, state):
        held, hidden = state
        held, hidden = layer(turn, entering(turn, held), hidden, own_weights)
        return move(held, opening_pairs(0) + opening_pairs(1)[1:]), hidden

    held, hidden = lax.fori_loop(0, 2, begin, (held, hidden))
    held, other_weights = lax.optimization_barrier((held, other_weights))
    all_weights = own_weights + other_weights
    for turn in range(2, groups + 1):
        if turn < groups:
            held = entering(turn, held)
        held, hidden = layer(turn, held, hidden, own_weights if turn < 3 else all_weights)
        held = move(held, opening_pairs(turn))

    def advance(i, state):
        held, hidden = state
        start = groups + 1 + 2 * i
        turns = lax.optimization_barrier((start, start + 1))
        for step, turn in enumerate(turns):
            held, hidden = layer(turn, held, hidden, all_weights)
            held = move(held, steady_pairs((groups + 2 + step) % 2))
        return held, hidden

    held, hidden = lax.fori_loop(0, (last - 2 - groups) // 2, advance, (held, hidden))
    for turn in (last - 1, last):
        held, hidden = layer(turn, held, hidden, all_weights)

    low, high = hidden[:groups], hidden[groups + 1 : 2 * groups + 1]
    theirs = jnp.where(column == 0, high[0::2], low[1::2])
    theirs = lax.ppermute(theirs, "section", swap)
    mine = jnp.where(column == 0, low, high)
    result = [
        jnp.where((stage == 0) | (column == j % 2), mine[j], theirs[j // 2]) for j in range(groups)
    ]
    return jnp.stack(result).reshape(1, micro, rows_one, parts * lanes)


def solution(mesh):
    in_specs = (
        P(None, "expert", "section"),
        P("section", None),
        P("section", "expert", None, None),
        P("section", "expert", None, None),
        P("section", "expert", None, None),
        P("section", None, "expert", None),
        P("section", None, "expert", None),
    )
    out_specs = P("section", None, "expert", None)
    return jax.shard_map(local, mesh=mesh, in_specs=in_specs, out_specs=out_specs, check_vma=False)
```

```python
import functools

import jax
import jax.numpy as jnp
from jax import lax
from jax.experimental import pallas as pl
from jax.experimental.pallas import tpu as pltpu
from jax.sharding import PartitionSpec as P

CAP = 2
EPS = 1e-06
LANES = 128
GROUP = 2

VMEM = pl.BlockSpec(memory_space=pltpu.VMEM)
SMEM = pl.BlockSpec(memory_space=pltpu.SMEM)
ANY = pl.BlockSpec(memory_space=pl.ANY)


def place_kernel(turn_ref, row_ref, x_ref, gain_ref, send_ref, normed_ref):
    experts, slots, parts, lanes = send_ref.shape
    wide = x_ref[...].astype(jnp.float32)
    mean = jnp.sum(wide * wide, axis=(1, 2), keepdims=True) * (1.0 / (parts * lanes))
    normed = wide * lax.rsqrt(mean + EPS) * gain_ref[...][None]
    normed_ref[...] = normed.astype(jnp.bfloat16)
    pick = turn_ref[0]
    for e in range(experts):
        for q in range(slots):
            send_ref[e, q] = normed_ref[row_ref[pick, e * slots + q]]


def expert_kernel(own_ref, recv_ref, *refs):
    out_ref, gate_ref, up_ref, down_ref, wide_ref, sems = refs[-6:]
    weights, held = refs[:-6], (gate_ref, up_ref, down_ref)
    rows, parts, lanes = recv_ref.shape
    copies = [pltpu.make_async_copy(weights[i], held[i], sems.at[i]) for i in range(3)]
    if len(weights) == 3:
        for copy in copies:
            copy.start()
    else:

        @pl.when(own_ref[0] == 1)
        def _():
            for copy in copies:
                copy.start()

        @pl.when(own_ref[0] != 1)
        def _():
            for i in range(3):
                pltpu.make_async_copy(weights[3 + i], held[i], sems.at[i]).start()

    wide_ref[...] = recv_ref[...].astype(jnp.float32).reshape(rows * parts, lanes)
    routed = jnp.concatenate(
        [wide_ref[pl.ds(c, rows, stride=parts), :].astype(jnp.bfloat16) for c in range(parts)],
        axis=1,
    )
    copies[0].wait()
    gate = jnp.dot(routed, gate_ref[...], preferred_element_type=jnp.float32)
    copies[1].wait()
    up = jnp.dot(routed, up_ref[...], preferred_element_type=jnp.float32)
    active = (gate / (1.0 + jnp.exp(-gate)) * up).astype(jnp.bfloat16)
    copies[2].wait()
    result = jnp.dot(active, down_ref[...], preferred_element_type=jnp.float32)
    for c in range(parts):
        wide_ref[pl.ds(c, rows, stride=parts), :] = result[:, c * lanes : (c + 1) * lanes]
    out_ref[...] = wide_ref[...].reshape(rows, parts, lanes).astype(jnp.bfloat16)


def mix_kernel(turn_ref, slot_ref, share_ref, ret_ref, x_ref, out_ref):
    rows = x_ref.shape[0]
    top = slot_ref.shape[1] // rows
    pick = turn_ref[0]
    for r in range(rows):
        total = x_ref[r].astype(jnp.float32)
        for k in range(top):
            part = ret_ref[slot_ref[pick, r * top + k]].astype(jnp.float32)
            total = total + share_ref[pick, r * top + k] * part
        out_ref[r] = total.astype(jnp.bfloat16)


def tables(expert_list, gate_probs, experts):
    micro, rows, _ = expert_list.shape
    groups = micro // GROUP
    number = jnp.arange(rows)
    member = (jnp.arange(micro) % GROUP)[:, None, None]
    chosen = expert_list[..., None] == jnp.arange(experts)
    named = chosen.any(axis=2)
    first = jnp.min(jnp.where(named, number[None, :, None], rows - 1), axis=1)
    last = jnp.max(jnp.where(named, number[None, :, None], 0), axis=1)
    later = chosen & (first[:, None, None, :] < number[None, :, None, None])
    rank = jnp.sum(later.astype(jnp.int32), axis=3)
    slot = expert_list * (CAP * GROUP) + member * CAP + rank
    source = jnp.stack([first, last], axis=2) + member * rows
    source = source.reshape(groups, GROUP, experts, CAP).transpose(0, 2, 1, 3)
    share = gate_probs / jnp.sum(gate_probs, axis=-1, keepdims=True)
    spare = lambda a: jnp.pad(a.reshape(groups, -1), ((0, 1), (0, 0)))
    return spare(source), spare(slot), spare(share)


def local(tokens, norm_gain, gate_weight, up_weight, down_weight, expert_ids, gate_probs):
    section = lax.axis_index("section")
    sections = lax.axis_size("section")
    experts = lax.axis_size("expert")
    column, stage = section % 2, section // 2
    micro, rows_one, lanes = tokens.shape
    groups = micro // GROUP
    rows = rows_one * GROUP
    parts = sections
    slots = CAP * GROUP
    last = sections + groups - 2
    swap = [(i, i ^ 1) for i in range(sections)]

    fresh = jnp.broadcast_to(tokens.reshape(1, -1, lanes), (sections, micro * rows_one, lanes))
    fresh = lax.all_to_all(fresh, "section", split_axis=0, concat_axis=0, tiled=True)
    fresh = fresh.transpose(1, 0, 2).reshape(groups, rows, parts, lanes)

    source, slot, share = tables(expert_ids[0], gate_probs[0], experts)
    gain = norm_gain.reshape(parts, lanes)
    flat = lambda a: a.reshape(-1, lanes).astype(jnp.float32)
    packed = jnp.concatenate([flat(source), flat(slot), flat(share), gain])
    moved = lax.ppermute(packed, "section", swap)
    both = jnp.where(column == 0, jnp.stack([packed, moved]), jnp.stack([moved, packed]))
    size = source.size // lanes
    as_table = lambda a: a.reshape(2 * (groups + 1), -1)
    source = as_table(both[:, :size]).astype(jnp.int32)
    slot = as_table(both[:, size : 2 * size]).astype(jnp.int32)
    share = as_table(both[:, 2 * size : 3 * size])
    gains = both[:, 3 * size :].reshape(2 * parts, lanes)

    own_weights = (gate_weight[0, 0], up_weight[0, 0], down_weight[0, 0])
    ready, fresh, gains = lax.optimization_barrier((own_weights, fresh, gains))
    other_weights = tuple(lax.ppermute(w, "section", swap[2:]) for w in ready)

    params = pltpu.CompilerParams(vmem_limit_bytes=24 * 1024 * 1024)
    bf = lambda *shape: jax.ShapeDtypeStruct(shape, jnp.bfloat16)
    place = pl.pallas_call(
        place_kernel,
        out_shape=bf(experts, slots, parts, lanes),
        in_specs=[SMEM, SMEM, VMEM, VMEM],
        out_specs=VMEM,
        scratch_shapes=[pltpu.VMEM((rows, parts, lanes), jnp.bfloat16)],
        compiler_params=params,
        name="place",
    )
    def expert(own, arrived, *weights):
        return pl.pallas_call(
            expert_kernel,
            out_shape=bf(experts * slots, parts, lanes),
            in_specs=[SMEM, VMEM] + [ANY] * len(weights),
            out_specs=VMEM,
            scratch_shapes=[pltpu.VMEM(w.shape, jnp.bfloat16) for w in own_weights]
            + [
                pltpu.VMEM((experts * slots * parts, lanes), jnp.float32),
                pltpu.SemaphoreType.DMA((3,)),
            ],
            compiler_params=params,
            name="expert",
        )(own, arrived, *weights)

    mix = pl.pallas_call(
        mix_kernel,
        out_shape=bf(rows, parts, lanes),
        in_specs=[SMEM, SMEM, SMEM, VMEM, VMEM],
        out_specs=VMEM,
        compiler_params=params,
        name="mix",
    )
    exchange = lambda a: lax.all_to_all(a, "expert", split_axis=0, concat_axis=0, tiled=True)

    def layer(turn, held, hidden, weights):
        turn, held, hidden = lax.optimization_barrier((jnp.int32(turn), held, hidden))
        second = jnp.where(stage == 0, column, (turn - column) % 2)
        group = turn - 2 * stage - second
        active = (group >= 0) & (group < groups)
        pick = (jnp.where(active, group, groups) + second * (groups + 1)).astype(jnp.int32)
        own = ((stage == 0) | (second == column)).astype(jnp.int32).reshape(1)
        at = pick.reshape(1)
        gain_now = lax.dynamic_slice_in_dim(gains, second * parts, parts, 0)
        at, pick, own, gain_now, held, hidden = lax.optimization_barrier(
            (at, pick, own, gain_now, held, hidden)
        )
        sent = place(at, source, held, gain_now)
        arrived = exchange(sent.reshape(experts, slots * parts, lanes))
        results = expert(own, arrived.reshape(experts * slots, parts, lanes), *weights)
        returned = exchange(results.reshape(experts, slots * parts, lanes))
        returned, pick = lax.optimization_barrier((returned, pick))
        output = mix(at, slot, share, returned.reshape(experts * slots, parts, lanes), held)
        return output, lax.dynamic_update_index_in_dim(hidden, output, pick, 0)

    def move(value, pairs):
        value, at = lax.optimization_barrier((value, section))
        here = functools.reduce(jnp.logical_or, [at == b for _, b in pairs])
        return jnp.where(here, lax.ppermute(value, "section", pairs), value)

    def opening_pairs(turn):
        pairs = [(0, 1)] if turn < groups else []
        pairs += [(1, 2 + (turn - 1) % 2)] if 1 <= turn <= groups else []
        for a in range(2, sections - 2):
            group = turn - (a // 2 * 2 + 1)
            if 0 <= group < groups and group % 2 == a % 2:
                pairs.append((a, a + 2))
        return pairs

    def steady_pairs(parity):
        return [(a, a + 2) for a in range(2 + parity, sections - 2, 2)]

    hidden = jnp.zeros((2 * (groups + 1), rows, parts, lanes), jnp.bfloat16)
    held = jnp.zeros((rows, parts, lanes), jnp.bfloat16)

    def entering(turn, held):
        group = lax.dynamic_index_in_dim(fresh, turn, 0, keepdims=False)
        return jnp.where(section == 0, group, held)

    def begin(turn, state):
        held, hidden = state
        held, hidden = layer(turn, entering(turn, held), hidden, own_weights)
        return move(held, opening_pairs(0) + opening_pairs(1)[1:]), hidden

    held, hidden = lax.fori_loop(0, 2, begin, (held, hidden))
    held, other_weights = lax.optimization_barrier((held, other_weights))
    all_weights = own_weights + other_weights
    for turn in range(2, groups + 1):
        if turn < groups:
            held = entering(turn, held)
        held, hidden = layer(turn, held, hidden, own_weights if turn < 3 else all_weights)
        held = move(held, opening_pairs(turn))

    def advance(i, state):
        held, hidden = state
        start = groups + 1 + 2 * i
        turns = lax.optimization_barrier((start, start + 1))
        for step, turn in enumerate(turns):
            held, hidden = layer(turn, held, hidden, all_weights)
            held = move(held, steady_pairs((groups + 2 + step) % 2))
        return held, hidden

    held, hidden = lax.fori_loop(0, (last - 2 - groups) // 2, advance, (held, hidden))
    held, hidden = layer(last - 1, held, hidden, all_weights)
    low, high = hidden[:groups], hidden[groups + 1 : 2 * groups + 1]
    theirs = jnp.where(column == 0, high[0::2], low[1::2])
    theirs = lax.ppermute(theirs, "section", swap)
    _, hidden = layer(last, held, hidden, all_weights)
    low, high = hidden[:groups], hidden[groups + 1 : 2 * groups + 1]
    mine = jnp.where(column == 0, low, high)
    result = [
        jnp.where((stage == 0) | (column == j % 2), mine[j], theirs[j // 2]) for j in range(groups)
    ]
    return jnp.stack(result).reshape(1, micro, rows_one, parts * lanes)


def solution(mesh):
    in_specs = (
        P(None, "expert", "section"),
        P("section", None),
        P("section", "expert", None, None),
        P("section", "expert", None, None),
        P("section", "expert", None, None),
        P("section", None, "expert", None),
        P("section", None, "expert", None),
    )
    out_specs = P("section", None, "expert", None)
    return jax.shard_map(local, mesh=mesh, in_specs=in_specs, out_specs=out_specs, check_vma=False)
```
